32 devices in a mesh: groups: 2 (over x), seq: 16 (over z, y, core).
Axes of the slice: x: 2, y: 2, z: 4, core: 2. Of those that a mesh axis runs over, the one named last changes fastest.
Arguments:
- queries: bfloat16 [8192, 1280], P(('groups', 'seq')), parts along dimension 0, may hold values from -6 to 6
- keys: bfloat16 [8192, 1280], P(('groups', 'seq')), parts along dimension 0, may hold values from -6 to 6
- values: bfloat16 [8192, 1280], P(('groups', 'seq')), parts along dimension 0, may hold values from -6 to 6
- cotangent: bfloat16 [8192, 1280], P(('groups', 'seq')), parts along dimension 0, may hold values from -6 to 6
- local_blocks: int32 [64, 3], P('groups'), parts along dimension 0, may hold values from -1 to 31, as said below
- far_blocks: int32 [64, 4], P('groups'), parts along dimension 0, may hold values from -1 to 29, as said below
- counts: int32 [64], P('groups'), parts along dimension 0, may hold values from 2 to 128
Outputs:
- attended: bfloat16 [8192, 1280], P(('groups', 'seq')), parts along dimension 0
- grad_queries: bfloat16 [8192, 1280], P(('groups', 'seq')), parts along dimension 0
- grad_keys: bfloat16 [8192, 1280], P(('groups', 'seq')), parts along dimension 0
- grad_values: bfloat16 [8192, 1280], P(('groups', 'seq')), parts along dimension 0
The draws below stay inside these ranges and needn't reach their ends.
There are 2 independent parts, one for each index of `groups`. The reference program is written for one: setup_inputs(seed, part) draws one part's arguments, and reference() takes and returns one part's arrays. A program takes and returns all parts, laid end to end along the dimension named above; each array names one. Nothing has to cross between parts.
Inputs may be any that keep to these rules, and one draw needn't show every extreme that they name: `local_blocks`: row b holds block b itself first, then 3 - 1 distinct blocks whose index differs from b by 1 to 2, or -1 where such a block lies outside the sequence. `far_blocks`: each entry of row b is -1 or a block whose index lies in [(b // 2 - k) * 2, (b // 2 - k + 1) * 2) for some k from 1 to 2; it is -1 exactly where that range would start below 0. Entries may repeat.
All inputs are finite; a program needn't handle non-finite values.
Results may differ from the reference program's by a relative error of at most 0.027.
Values may be sent and summed in bfloat16 or wider, within the bound.
A program may use at most 128 MiB of HBM per device.

```python
import math
import jax
import jax.numpy as jnp
from jax import lax

D = 1280
HEADS = 16
BLK = 128
LR = 2
NLOC = 3
NFAR = 4
HOPS = 2
TOKENS = 4096
NBLK = 32
NB_DEV = 2


def background(key, marker):
    return jnp.clip(jax.random.normal(jax.random.fold_in(key, marker), (TOKENS, D)), -6.0, 6.0)


def draw_queries(key, part):
    drawn = background(key, 1).reshape(NBLK, BLK, D)
    return drawn.reshape(TOKENS, D).astype(jnp.bfloat16)


def draw_keys(key, part):
    drawn = background(key, 5).reshape(NBLK, BLK, D)
    return drawn.reshape(TOKENS, D).astype(jnp.bfloat16)


def draw_local_blocks(key, part):
    others = jnp.concatenate((jnp.arange(-LR, 0, dtype=jnp.int32), jnp.arange(1, LR + 1, dtype=jnp.int32)))
    ranking = jax.random.randint(jax.random.fold_in(key, 11), (NBLK, 2 * LR), 0, 1 << 20)
    ordering = jnp.argsort(ranking, axis=1, stable=True)
    picked = others[ordering[:, :NLOC - 1]]
    offsets = jnp.concatenate((jnp.zeros((NBLK, 1), jnp.int32), picked), axis=1)
    target = jnp.arange(NBLK, dtype=jnp.int32)[:, None] + offsets
    return jnp.where((target >= 0) & (target < NBLK), target, -1).astype(jnp.int32)


def draw_far_blocks(key, part):
    hop_count = jax.random.randint(jax.random.fold_in(key, 21), (NBLK, NFAR), 1, HOPS + 1)
    within = jax.random.randint(jax.random.fold_in(key, 22), (NBLK, NFAR), 0, NB_DEV)
    source = jnp.arange(NBLK, dtype=jnp.int32)[:, None] // NB_DEV - hop_count
    return jnp.where(source >= 0, source * NB_DEV + within, -1).astype(jnp.int32)


def place_ends(values, rng, smallest, high):
    spot = [jax.random.randint(jax.random.fold_in(rng, axis), (), 0, length) for axis, length in enumerate(values.shape)]
    main_axis = values.shape.index(max(values.shape))
    beside = spot[:main_axis] + [(spot[main_axis] + 1) % values.shape[main_axis]] + spot[main_axis + 1:]
    return values.at[tuple(spot)].set(smallest).at[tuple(beside)].set(high)


def levels(stream_key, shape, pieces, least, largest):
    loudness = 1.0
    for dim, shards_of in pieces:
        heights = jax.random.uniform(jax.random.fold_in(jax.random.fold_in(stream_key, 6), dim), (shards_of,), jnp.float32, least / len(pieces), largest / len(pieces))
        loudness = loudness * jnp.repeat(jnp.exp(heights), shape[dim] // shards_of).reshape((-1,) + (1,) * (len(shape) - 1 - dim))
    return loudness


def noise(rng, shape, scale, reach, shards=(), held_as=jnp.bfloat16):
    values = jax.random.normal(rng, shape, jnp.float32) * scale
    if len(shards) > 0:
        values = levels(rng, shape, shards, -0.22, 0.18) * values
    return jnp.clip(values, min=-reach, max=reach).astype(held_as)


def setup_inputs(seed: int = 0, part: int = 0) -> dict:
    splits = jax.random.split(jax.random.key(seed), 8)
    part_keys = jax.random.split(jax.random.fold_in(splits[7], part), 8)
    return {
        "queries": draw_queries(jax.random.fold_in(jax.random.fold_in(splits[7], part), 71), part),
        "keys": draw_keys(jax.random.fold_in(jax.random.fold_in(splits[7], part), 71), part),
        "values": noise(part_keys[2], (TOKENS, D), 1.0, 6.0, ((0, 16),)),
        "cotangent": noise(part_keys[3], (TOKENS, D), 1.0, 6.0, ((0, 16),)),
        "local_blocks": draw_local_blocks(jax.random.fold_in(jax.random.fold_in(splits[7], part), 71), part),
        "far_blocks": draw_far_blocks(jax.random.fold_in(jax.random.fold_in(splits[7], part), 71), part),
        "counts": place_ends(jax.random.randint(part_keys[6], (NBLK,), 2, BLK + 1), jax.random.fold_in(part_keys[6], 1), 2, BLK).astype(jnp.int32),
    }


def reference(queries, keys, values, cotangent, local_blocks, far_blocks, counts):
    total_rows, model_width = queries.shape
    head_size = model_width // HEADS
    block_total = total_rows // BLK
    slot_total = NLOC + NFAR
    score_scale = 1.0 / math.sqrt(head_size)
    highest = lax.Precision.HIGHEST
    listing = jnp.concatenate((local_blocks, far_blocks), axis=1).astype(jnp.int32)
    position = jnp.arange(BLK, dtype=jnp.int32)
    slot_order = jnp.arange(slot_total, dtype=jnp.int32)

    def one_block(carried, block_id):
        key_sums, value_sums = carried
        chosen = lax.dynamic_index_in_dim(listing, block_id, 0, keepdims=False)
        repeated = jnp.any((chosen[:, None] == chosen[None, :]) & (slot_order[None, :] < slot_order[:, None]), axis=1)
        slot_live = (chosen >= 0) & jnp.logical_not(repeated)
        safe_index = jnp.maximum(chosen, 0).astype(jnp.int32)
        key_count = counts[safe_index]
        key_mask = (slot_live[:, None] & (position[None, :] < key_count[:, None])).reshape(-1)
        key_rows = (safe_index[:, None] * BLK + position[None, :]).reshape(-1).astype(jnp.int32)
        near_keys = keys[key_rows].astype(jnp.float32).reshape(-1, HEADS, head_size)
        near_values = values[key_rows].astype(jnp.float32).reshape(-1, HEADS, head_size)
        first_row = (block_id * BLK).astype(jnp.int32)
        block_query = lax.dynamic_slice_in_dim(queries, first_row, BLK, 0).astype(jnp.float32).reshape(BLK, HEADS, head_size)
        block_grad = lax.dynamic_slice_in_dim(cotangent, first_row, BLK, 0).astype(jnp.float32)
        grad_heads = block_grad.reshape(BLK, HEADS, head_size)
        scores = jnp.einsum('qhd,khd->hqk', block_query, near_keys, precision=highest) * score_scale
        masked = jnp.where(key_mask[None, None, :], scores, -jnp.inf)
        row_peak = lax.optimization_barrier(jnp.max(masked, axis=2, keepdims=True))
        row_total = lax.optimization_barrier(jnp.sum(jnp.where(key_mask[None, None, :], jnp.exp(scores - row_peak), 0.0), axis=2, keepdims=True))
        log_total = row_peak + jnp.log(row_total)
        chance = jnp.where(key_mask[None, None, :], jnp.exp(scores - log_total), 0.0)
        weights = lax.optimization_barrier(chance.astype(jnp.bfloat16)).astype(jnp.float32)
        block_out = jnp.einsum('hqk,khd->qhd', weights, near_values, precision=highest).reshape(BLK, model_width).astype(jnp.bfloat16)
        out_wide = lax.optimization_barrier(block_out).astype(jnp.float32)
        row_delta = lax.optimization_barrier(jnp.sum((block_grad * out_wide).reshape(BLK, HEADS, head_size), axis=2)).T
        grad_chance = jnp.einsum('qhd,khd->hqk', grad_heads, near_values, precision=highest)
        grad_scores = chance * (grad_chance - row_delta[:, :, None])
        grad_scores = lax.optimization_barrier(grad_scores.astype(jnp.bfloat16)).astype(jnp.float32)
        query_part = (jnp.einsum('hqk,khd->qhd', grad_scores, near_keys, precision=highest) * score_scale).reshape(BLK, model_width).astype(jnp.bfloat16)
        key_part = (jnp.einsum('hqk,qhd->khd', grad_scores, block_query, precision=highest) * score_scale).reshape(-1, model_width)
        value_part = jnp.einsum('hqk,qhd->khd', weights, grad_heads, precision=highest).reshape(-1, model_width)
        key_sums = key_sums.at[key_rows].add(key_part)
        value_sums = value_sums.at[key_rows].add(value_part)
        return ((key_sums, value_sums), (block_out, query_part))
    empty = jnp.zeros((total_rows, model_width), jnp.float32)
    sums, outputs = lax.scan(one_block, (empty, empty), jnp.arange(block_total, dtype=jnp.int32))
    attended = outputs[0].reshape(total_rows, model_width)
    grad_queries = outputs[1].reshape(total_rows, model_width)
    return (attended, grad_queries, sums[0].astype(jnp.bfloat16), sums[1].astype(jnp.bfloat16))
```

```python
import functools
import math

import jax
import jax.numpy as jnp
from jax import lax
from jax.experimental import pallas as pl
from jax.experimental.pallas import tpu as pltpu
from jax.sharding import PartitionSpec as P

HEADS = 16
BLK = 128
MESH = pl.DeviceIdType.MESH
OFF = -1e30
NCH = 2
BF = jnp.bfloat16
F32 = jnp.float32


def dot_nt(a, b):
    return lax.dot_general(a, b, (((1,), (1,)), ((), ())), preferred_element_type=F32)


def dot_nn(a, b):
    return lax.dot_general(a, b, (((1,), (0,)), ((), ())), preferred_element_type=F32)


def dot_tn(a, b):
    return lax.dot_general(a, b, (((0,), (0,)), ((), ())), preferred_element_type=F32)


def kernel(
    n, q_hbm, k_hbm, v_hbm, g_hbm, local_ref, far_ref, counts_ref,
    o_ref, dq_ref, dk_ref, dv_ref,
    kbuf, vbuf, qbuf, gbuf, bias, acc, own, oacc, gsend, grecv,
    own_sem, kv_send, kv_recv, gr_send, gr_recv,
):
    d = lax.axis_index("seq")
    even = lax.rem(d, 2) == 0
    rows, width = q_hbm.shape
    cols = width // NCH
    head = width // HEADS
    hpc = HEADS // NCH
    blocks = rows // BLK
    nblk = counts_ref.shape[0]
    hbm = (k_hbm, v_hbm)
    bufs = (kbuf, vbuf)
    scale = 1.0 / math.sqrt(head)

    def part(ref, c):
        return ref.at[:, pl.ds(pl.multiple_of(c * cols, 128), cols)]

    def slot(a, c, s):
        return bufs[a].at[c, pl.ds(s * rows, rows), :]

    def own_copies(c):
        out = []
        for i, (src, dst) in enumerate(
            ((k_hbm, slot(0, c, 2)), (v_hbm, slot(1, c, 2)), (q_hbm, qbuf.at[c]), (g_hbm, gbuf.at[c]))
        ):
            out.append(pltpu.make_async_copy(part(src, c), dst, own_sem.at[c, i]))
        return out

    def remote(src, dst, send, recv, target):
        return pltpu.make_async_remote_copy(
            src_ref=src, dst_ref=dst, send_sem=send, recv_sem=recv,
            device_id={"seq": target}, device_id_type=MESH,
        )

    def kv_copy(kind, a, c):
        dst_slot = (1, 3, 0, 0)[kind]
        target = (d + 1, d - 1, d + 2, d + 1)[kind]
        src = slot(a, c, 1) if kind == 3 else part(hbm[a], c)
        return remote(
            src, slot(a, c, dst_slot), kv_send.at[c, kind, a],
            kv_recv.at[c, (0, 1, 0, 2)[dst_slot], a], target,
        )

    has_prev = d >= 1
    has_prev2 = d >= 2
    has_next = d + 1 < n
    has_next2 = d + 2 < n
    kv_cond = (has_next, has_prev, even & has_next2, even & has_prev2)
    in_cond = (has_prev2, has_prev, has_next)

    def kv_arrived(place, a, c):
        s = (0, 1, 3)[place]
        return remote(slot(a, c, s), slot(a, c, s), kv_send.at[c, 0, a], kv_recv.at[c, place, a], d)

    def gr_copy(kind, to_place, target, a, c):
        return remote(
            gsend.at[c, kind, a], grecv.at[c, to_place, a], gr_send.at[c, kind, a],
            gr_recv.at[c, to_place, a], target,
        )

    barrier = pltpu.get_barrier_semaphore()
    peers = (
        (has_prev, d - 1), (has_next, d + 1),
        (even & has_prev2, d - 2), (even & has_next2, d + 2),
    )
    total = 0
    for cond, target in peers:
        total = total + cond.astype(jnp.int32)

        @pl.when(cond)
        def _(target=target):
            pl.semaphore_signal(barrier, inc=1, device_id={"seq": target}, device_id_type=MESH)

    def start_own(c, carry):
        for copy in own_copies(c):
            copy.start()
        return carry

    lax.fori_loop(0, NCH, start_own, 0)
    pl.semaphore_wait(barrier, total)

    def start_kv(c, carry):
        for kind in (2, 0, 1):
            @pl.when(kv_cond[kind])
            def _(kind=kind):
                for a in range(2):
                    kv_copy(kind, a, c).start()
        return carry

    lax.fori_loop(0, NCH, start_kv, 0)

    for place, s in ((0, 0), (1, 1), (2, 3)):
        @pl.when(jnp.logical_not(in_cond[place]))
        def _(s=s):
            for a in range(2):
                for c in range(NCH):
                    bufs[a][c, pl.ds(s * rows, rows), :] = jnp.zeros((rows, cols), BF)

    position = lax.broadcasted_iota(jnp.int32, (BLK, BLK), 0)
    first = d * blocks
    for e in range(4 * blocks):
        index = first - 2 * blocks + e
        inside = (index >= 0) & (index < nblk)
        count = counts_ref[jnp.clip(index, 0, nblk - 1)]
        for a in range(blocks):
            listed = local_ref[first + a, 0] == index
            for s in range(1, local_ref.shape[1]):
                listed = listed | (local_ref[first + a, s] == index)
            for s in range(far_ref.shape[1]):
                listed = listed | (far_ref[first + a, s] == index)
            live = jnp.where(listed & inside, count, 0)
            bias[pl.ds(e * BLK, BLK), pl.ds(a * BLK, BLK)] = jnp.where(position < live, 0.0, OFF)

    def compute(c):
        done = set()
        for h in range(hpc):
            low = h * head
            w0 = low // 128 * 128
            w1 = -(-(low + head) // 128) * 128
            w = w1 - w0
            lane = lax.broadcasted_iota(jnp.int32, (1, w), 1) + w0
            inhead = ((lane >= low) & (lane < low + head)).astype(F32)
            inhead_b = inhead.astype(BF)
            win = pl.ds(w0, w)
            qm = qbuf[c, :, win] * inhead_b
            gm = gbuf[c, :, win] * inhead_b
            kw = kbuf[c, :, win]
            vw = vbuf[c, :, win]
            s = dot_nt(kw, qm) * (scale * math.log2(math.e)) + bias[...]
            peak = jnp.max(s, axis=0, keepdims=True)
            e = jnp.exp2(s - peak)
            inv = 1.0 / jnp.sum(e, axis=0, keepdims=True)
            p = e * inv
            dp = dot_nt(vw, gm)
            delta = jnp.sum(p * dp, axis=0, keepdims=True)
            pb = p.astype(BF)
            ds = (p * (dp - delta)).astype(BF)
            terms = (
                (oacc, 0, dot_tn(pb, vw) * inhead),
                (oacc, 1, dot_tn(ds, kw) * inhead),
                (acc, 0, dot_nn(ds, qm)),
                (acc, 1, dot_nn(pb, gm)),
            )
            for ref, i, term in terms:
                for t in range(w0, w1, 128):
                    piece = term[:, t - w0 : t - w0 + 128]
                    at = pl.ds(t, 128)
                    if t in done:
                        ref[i, :, at] += piece
                    else:
                        ref[i, :, at] = piece
            done.update(range(w0, w1, 128))
        at = pl.ds(pl.multiple_of(c * cols, 128), cols)
        o_ref[:, at] = oacc[0].astype(BF)
        dq_ref[:, at] = (oacc[1] * scale).astype(BF)
        for a in range(2):
            f = scale if a == 0 else 1.0
            for kind, s in ((0, 0), (1, 1), (2, 3)):
                gsend[c, kind, a] = (acc[a, pl.ds(s * rows, rows), :] * f).astype(BF)
            own[c, a] = acc[a, pl.ds(2 * rows, rows), :] * f

    def chunk(c, carry):
        @pl.when(has_prev)
        def _():
            for a in range(2):
                kv_arrived(1, a, c).wait_recv()

        @pl.when(kv_cond[3])
        def _():
            for a in range(2):
                kv_copy(3, a, c).start()

        for place in (0, 2):
            @pl.when(in_cond[place])
            def _(place=place):
                for a in range(2):
                    kv_arrived(place, a, c).wait_recv()

        for copy in own_copies(c):
            copy.wait()
        compute(c)

        @pl.when(even)
        def _():
            for a in range(2):
                @pl.when(has_prev2)
                def _(a=a):
                    gr_copy(0, 0, d - 2, a, c).start()
                gr_copy(2, 2, d + 1, a, c).start()

            @pl.when(has_prev2)
            def _():
                for a in range(2):
                    gr_copy(0, 3, d, a, c).wait_recv()
                    gsend[c, 1, a] = (
                        gsend[c, 1, a].astype(F32) + grecv[c, 3, a].astype(F32)
                    ).astype(BF)
                    gr_copy(1, 1, d - 1, a, c).start()

        @pl.when(jnp.logical_not(even))
        def _():
            @pl.when(has_prev2)
            def _():
                for a in range(2):
                    gr_copy(0, 3, d - 1, a, c).start()

            @pl.when(has_next)
            def _():
                for a in range(2):
                    gr_copy(2, 2, d + 1, a, c).start()
            for a in range(2):
                gr_copy(1, 1, d - 1, a, c).start()

        return carry

    lax.fori_loop(0, NCH, chunk, 0)

    def finish(c, carry):
        at = pl.ds(pl.multiple_of(c * cols, 128), cols)
        for place, cond in ((2, has_prev), (0, even & has_next2), (1, has_next)):
            @pl.when(cond)
            def _(place=place):
                for a in range(2):
                    gr_copy(0, place, d, a, c).wait_recv()
                    own[c, a] += grecv[c, place, a].astype(F32)
        dk_ref[:, at] = own[c, 0].astype(BF)
        dv_ref[:, at] = own[c, 1].astype(BF)
        for kind in range(4):
            @pl.when(kv_cond[kind])
            def _(kind=kind):
                for a in range(2):
                    kv_copy(kind, a, c).wait_send()
        for kind, cond in ((0, has_prev2), (1, has_prev), (2, has_next)):
            @pl.when(cond)
            def _(kind=kind):
                for a in range(2):
                    gr_copy(kind, kind, d, a, c).wait_send()
        return carry

    lax.fori_loop(0, NCH, finish, 0)


def body(queries, keys, values, cotangent, local_blocks, far_blocks, counts):
    rows, width = queries.shape
    cols = width // NCH
    n = lax.axis_size("seq")
    window = 4 * rows
    out = jax.ShapeDtypeStruct((rows, width), BF)
    any_spec = pl.BlockSpec(memory_space=pl.ANY)
    vmem = pl.BlockSpec(memory_space=pltpu.VMEM)
    smem = pl.BlockSpec(memory_space=pltpu.SMEM)
    dma = pltpu.SemaphoreType.DMA
    return pl.pallas_call(
        functools.partial(kernel, n),
        out_shape=(out,) * 4,
        in_specs=[any_spec] * 4 + [smem] * 3,
        out_specs=(vmem,) * 4,
        scratch_shapes=[
            pltpu.VMEM((NCH, window, cols), BF),
            pltpu.VMEM((NCH, window, cols), BF),
            pltpu.VMEM((NCH, rows, cols), BF),
            pltpu.VMEM((NCH, rows, cols), BF),
            pltpu.VMEM((window, rows), F32),
            pltpu.VMEM((2, window, cols), F32),
            pltpu.VMEM((NCH, 2, rows, cols), F32),
            pltpu.VMEM((2, rows, cols), F32),
            pltpu.VMEM((NCH, 3, 2, rows, cols), BF),
            pltpu.VMEM((NCH, 4, 2, rows, cols), BF),
            dma((NCH, 4)),
            dma((NCH, 4, 2)),
            dma((NCH, 3, 2)),
            dma((NCH, 3, 2)),
            dma((NCH, 4, 2)),
        ],
        compiler_params=pltpu.CompilerParams(
            collective_id=0, has_side_effects=True, vmem_limit_bytes=56 * 1024 * 1024
        ),
        name="attention",
    )(queries, keys, values, cotangent, local_blocks, far_blocks, counts)


def solution(mesh):
    rows = P(("groups", "seq"), None)
    return jax.shard_map(
        body,
        mesh=mesh,
        in_specs=(rows, rows, rows, rows, P("groups", None), P("groups", None), P("groups")),
        out_specs=(rows,) * 4,
        check_vma=False,
    )
```

```python
import functools
import math

import jax
import jax.numpy as jnp
from jax import lax
from jax.experimental import pallas as pl
from jax.experimental.pallas import tpu as pltpu
from jax.sharding import PartitionSpec as P

HEADS = 16
BLK = 128
MESH = pl.DeviceIdType.MESH
OFF = -1e30
NCH = 2
BF = jnp.bfloat16
F32 = jnp.float32


def dot_nt(a, b):
    return lax.dot_general(a, b, (((1,), (1,)), ((), ())), preferred_element_type=F32)


def dot_nn(a, b):
    return lax.dot_general(a, b, (((1,), (0,)), ((), ())), preferred_element_type=F32)


def dot_tn(a, b):
    return lax.dot_general(a, b, (((0,), (0,)), ((), ())), preferred_element_type=F32)


def kernel(
    n, q_hbm, k_hbm, v_hbm, g_hbm, local_ref, far_ref, counts_ref,
    o_ref, dq_ref, dk_ref, dv_ref,
    kbuf, vbuf, qbuf, gbuf, bias, acc, own, oacc, gsend, grecv,
    transit, own_sem, kv_send, kv_recv, gr_send, gr_recv,
):
    d = lax.axis_index("seq")
    place4 = lax.rem(d, 4)
    r0, r1, r2, r3 = (place4 == i for i in range(4))
    even = r0 | r2
    odd = r1 | r3
    rows, width = q_hbm.shape
    cols = width // NCH
    head = width // HEADS
    hpc = HEADS // NCH
    blocks = rows // BLK
    nblk = counts_ref.shape[0]
    hbm = (k_hbm, v_hbm)
    bufs = (kbuf, vbuf)
    scale = 1.0 / math.sqrt(head)
    early = 4
    cut = -(-(early * head) // 128) * 128
    spans = ((0, cut), (cut, cols - cut))

    def slot(a, c, s):
        return bufs[a].at[c, pl.ds(s * rows, rows), :]

    def span(ref, p):
        return ref.at[:, pl.ds(spans[p][0], spans[p][1])]

    def part(ref, c, p):
        return ref.at[:, pl.ds(pl.multiple_of(c * cols + spans[p][0], 128), spans[p][1])]

    def own_copies(c, p):
        out = []
        for i, (src, dst) in enumerate(
            ((k_hbm, slot(0, c, 2)), (v_hbm, slot(1, c, 2)), (q_hbm, qbuf.at[c]), (g_hbm, gbuf.at[c]))
        ):
            out.append(pltpu.make_async_copy(part(src, c, p), span(dst, p), own_sem.at[c, p, i]))
        return out

    def remote(src, dst, send, recv, delta):
        return pltpu.make_async_remote_copy(
            src_ref=src, dst_ref=dst, send_sem=send, recv_sem=recv,
            device_id={"seq": d + delta}, device_id_type=MESH,
        )

    def landing(place, a, c, p):
        return span(transit.at[c, a] if place == 3 else slot(a, c, (0, 1, 3)[place]), p)

    def kv_send_all(kind, src_place, dst_place, delta, c, p):
        for a in range(2):
            src = part(hbm[a], c, p) if src_place is None else landing(src_place, a, c, p)
            remote(
                src, landing(dst_place, a, c, p), kv_send.at[c, p, kind, a],
                kv_recv.at[c, p, dst_place, a], delta,
            ).start()

    def kv_wait(place, c, p):
        for a in range(2):
            there = landing(place, a, c, p)
            remote(there, there, kv_send.at[c, p, 0, a], kv_recv.at[c, p, place, a], 0).wait_recv()

    def kv_wait_send(kind, c, p):
        for a in range(2):
            there = landing(0, a, c, p)
            remote(there, there, kv_send.at[c, p, kind, a], kv_recv.at[c, p, 0, a], 0).wait_send()

    def gr_send_all(kind, place, delta, c, p):
        for a in range(2):
            src = grecv.at[c, 2, a] if kind == 3 else gsend.at[c, kind, a]
            remote(
                span(src, p), span(grecv.at[c, place, a], p), gr_send.at[c, p, kind, a],
                gr_recv.at[c, p, place, a], delta,
            ).start()

    def gr_wait(place, c, p):
        for a in range(2):
            there = span(grecv.at[c, place, a], p)
            remote(there, there, gr_send.at[c, p, 0, a], gr_recv.at[c, p, place, a], 0).wait_recv()

    def gr_wait_send(kind, c, p):
        for a in range(2):
            there = span(grecv.at[c, 0, a], p)
            remote(there, there, gr_send.at[c, p, kind, a], gr_recv.at[c, p, 0, a], 0).wait_send()

    has_prev = d >= 1
    has_prev2 = d >= 2
    has_next = d + 1 < n
    low4 = d >= 4
    up4 = d + 4 < n
    up3 = d + 3 < n
    in_cond = (has_prev2, has_prev, has_next)
    k2_cond = (r0 & up4) | (r1 & up3) | (r2 & low4)
    k3_cond = (r0 & low4) | r2
    kv_cond = (even | odd, jnp.logical_not(r3) | has_next, k2_cond, k3_cond)

    barrier = pltpu.get_barrier_semaphore()
    total = 0
    for delta, who in (
        (1, r0 | r1 | r2), (-1, r1 | r2 | r3), (2, r0), (-2, r2),
        (3, r0 | r1 | r3), (-3, r0 | r2 | r3), (4, r0), (-4, r0),
    ):
        cond = who & (d + delta >= 0) & (d + delta < n)
        total = total + cond.astype(jnp.int32)

        @pl.when(cond)
        def _(delta=delta):
            pl.semaphore_signal(barrier, inc=1, device_id={"seq": d + delta}, device_id_type=MESH)

    def start_own(c, carry):
        for p in range(2):
            for copy in own_copies(c, p):
                copy.start()
        return carry

    lax.fori_loop(0, NCH, start_own, 0)
    pl.semaphore_wait(barrier, total)

    def start_kv(c, carry):
        for p in range(2):
            pl.when(r0)(lambda: kv_send_all(1, None, 0, 2, c, p))
            pl.when(r1)(lambda: kv_send_all(1, None, 1, 1, c, p))
            pl.when(r2)(lambda: kv_send_all(1, None, 2, -1, c, p))
            pl.when(r3 & has_next)(lambda: kv_send_all(1, None, 3, -3, c, p))
            pl.when(even)(lambda: kv_send_all(0, None, 1, 1, c, p))
            pl.when(odd)(lambda: kv_send_all(0, None, 2, -1, c, p))
        return carry

    lax.fori_loop(0, NCH, start_kv, 0)

    def hand_on(c, p):
        @pl.when(r0 & up4)
        def _():
            kv_wait(3, c, p)
            kv_send_all(2, 3, 1, 4, c, p)

        @pl.when(r1)
        def _():
            kv_wait(2, c, p)
            pl.when(up3)(lambda: kv_send_all(2, 2, 0, 3, c, p))

        @pl.when(r2)
        def _():
            kv_wait(0, c, p)
            pl.when(low4)(lambda: kv_send_all(2, 0, 2, -3, c, p))
            kv_wait(1, c, p)
            kv_send_all(3, 1, 0, 1, c, p)

    def arrive(c, p):
        @pl.when(r0 & low4)
        def _():
            kv_wait(1, c, p)
            kv_send_all(3, 1, 0, 1, c, p)
            kv_wait(0, c, p)
        pl.when(even)(lambda: kv_wait(2, c, p))
        pl.when(odd)(lambda: kv_wait(1, c, p))
        pl.when(odd & has_prev2)(lambda: kv_wait(0, c, p))
        pl.when(r3 & has_next)(lambda: kv_wait(2, c, p))
        for copy in own_copies(c, p):
            copy.wait()

    def add_in(kind, place, c, p):
        at = pl.ds(spans[p][0], spans[p][1])
        gr_wait(place, c, p)
        for a in range(2):
            gsend[c, kind, a, :, at] = (
                gsend[c, kind, a, :, at].astype(F32) + grecv[c, place, a, :, at].astype(F32)
            ).astype(BF)

    def emit(c, p):
        at = pl.ds(spans[p][0], spans[p][1])
        for a in range(2):
            f = scale if a == 0 else 1.0
            for kind, s in ((0, 0), (1, 1), (2, 3)):
                gsend[c, kind, a, :, at] = (acc[a, pl.ds(s * rows, rows), at] * f).astype(BF)
            own[c, a, :, at] = acc[a, pl.ds(2 * rows, rows), at] * f
        pl.when(r0 & low4)(lambda: gr_send_all(0, 2, -3, c, p))
        pl.when(odd & has_prev2)(lambda: gr_send_all(0, 3, -1, c, p))
        pl.when(r3 & has_next)(lambda: gr_send_all(2, 2, 3, c, p))
        pl.when(even)(lambda: gr_send_all(2, 0, 1, c, p))
        pl.when(odd)(lambda: gr_send_all(1, 0, -1, c, p))

    def combine(c, p):
        @pl.when(r0 & low4)
        def _():
            add_in(1, 3, c, p)
            gr_send_all(1, 2, -4, c, p)

        @pl.when(r1)
        def _():
            pl.when(up3)(lambda: add_in(2, 2, c, p))
            gr_send_all(2, 1, 1, c, p)

        @pl.when(r2)
        def _():
            add_in(1, 3, c, p)
            gr_send_all(1, 1, -1, c, p)
            pl.when(low4)(lambda: add_in(0, 2, c, p))
            gr_send_all(0, 1, -2, c, p)

    def pass_back(c, p):
        @pl.when(r0 & up4)
        def _():
            gr_wait(2, c, p)
            gr_send_all(3, 1, 3, c, p)

    hand_on(0, 0)

    for place, s in ((0, 0), (1, 1), (2, 3)):
        @pl.when(jnp.logical_not(in_cond[place]))
        def _(s=s):
            for a in range(2):
                for c in range(NCH):
                    bufs[a][c, pl.ds(s * rows, rows), :] = jnp.zeros((rows, cols), BF)

    position = lax.broadcasted_iota(jnp.int32, (BLK, BLK), 0)
    first = d * blocks
    for e in range(4 * blocks):
        index = first - 2 * blocks + e
        inside = (index >= 0) & (index < nblk)
        count = counts_ref[jnp.clip(index, 0, nblk - 1)]
        for a in range(blocks):
            listed = local_ref[first + a, 0] == index
            for s in range(1, local_ref.shape[1]):
                listed = listed | (local_ref[first + a, s] == index)
            for s in range(far_ref.shape[1]):
                listed = listed | (far_ref[first + a, s] == index)
            live = jnp.where(listed & inside, count, 0)
            bias[pl.ds(e * BLK, BLK), pl.ds(a * BLK, BLK)] = jnp.where(position < live, 0.0, OFF)

    hand_on(0, 1)

    def compute(c):
        done = set()
        for h in range(hpc):
            if h == 0:
                arrive(c, 0)
            if h == early:
                pl.when(c == 0)(lambda: hand_on(1, 0))
                pl.when(c == 1)(lambda: combine(0, 0))
                arrive(c, 1)
            if h == early + 1:
                emit(c, 0)
                pl.when(c == 0)(lambda: hand_on(1, 1))

                @pl.when(c == 1)
                def _():
                    combine(0, 1)
                    pass_back(0, 0)
            low = h * head
            w0 = low // 128 * 128
            w1 = -(-(low + head) // 128) * 128
            w = w1 - w0
            lane = lax.broadcasted_iota(jnp.int32, (1, w), 1) + w0
            inhead = ((lane >= low) & (lane < low + head)).astype(F32)
            inhead_b = inhead.astype(BF)
            win = pl.ds(w0, w)
            qm = qbuf[c, :, win] * inhead_b
            gm = gbuf[c, :, win] * inhead_b
            kw = kbuf[c, :, win]
            vw = vbuf[c, :, win]
            s = dot_nt(kw, qm) * (scale * math.log2(math.e)) + bias[...]
            peak = jnp.max(s, axis=0, keepdims=True)
            e = jnp.exp2(s - peak)
            inv = 1.0 / jnp.sum(e, axis=0, keepdims=True)
            p = e * inv
            dp = dot_nt(vw, gm)
            delta = jnp.sum(p * dp, axis=0, keepdims=True)
            pb = p.astype(BF)
            ds = (p * (dp - delta)).astype(BF)
            terms = (
                (oacc, 0, dot_tn(pb, vw) * inhead),
                (oacc, 1, dot_tn(ds, kw) * inhead),
                (acc, 0, dot_nn(ds, qm)),
                (acc, 1, dot_nn(pb, gm)),
            )
            for ref, i, term in terms:
                for t in range(w0, w1, 128):
                    piece = term[:, t - w0 : t - w0 + 128]
                    at = pl.ds(t, 128)
                    if t in done:
                        ref[i, :, at] += piece
                    else:
                        ref[i, :, at] = piece
            done.update(range(w0, w1, 128))
        at = pl.ds(pl.multiple_of(c * cols, 128), cols)
        o_ref[:, at] = oacc[0].astype(BF)
        dq_ref[:, at] = (oacc[1] * scale).astype(BF)

    def chunk(c, carry):
        compute(c)
        emit(c, 1)
        return carry

    lax.fori_loop(0, NCH, chunk, 0)

    combine(1, 0)
    pass_back(0, 1)
    combine(1, 1)
    pass_back(1, 0)

    def finish(c, carry):
        pl.when(c == 1)(lambda: pass_back(1, 1))
        at = pl.ds(pl.multiple_of(c * cols, 128), cols)
        for p in range(2):
            gr_wait(0, c, p)
            pl.when(jnp.logical_not(r3) | has_next)(lambda: gr_wait(1, c, p))
        for a, ref in ((0, dk_ref), (1, dv_ref)):
            mine = own[c, a] + grecv[c, 0, a].astype(F32)
            other = grecv[c, 1, a].astype(F32)
            ref[:, at] = (mine + jnp.where(jnp.logical_not(r3) | has_next, other, 0.0)).astype(BF)
        for p in range(2):
            for kind in range(4):
                pl.when(kv_cond[kind])(lambda: kv_wait_send(kind, c, p))
            for kind, cond in ((0, has_prev2), (1, has_prev), (2, has_next), (3, r0 & up4)):
                pl.when(cond)(lambda: gr_wait_send(kind, c, p))
        return carry

    lax.fori_loop(0, NCH, finish, 0)


def body(queries, keys, values, cotangent, local_blocks, far_blocks, counts):
    rows, width = queries.shape
    cols = width // NCH
    n = lax.axis_size("seq")
    window = 4 * rows
    out = jax.ShapeDtypeStruct((rows, width), BF)
    any_spec = pl.BlockSpec(memory_space=pl.ANY)
    vmem = pl.BlockSpec(memory_space=pltpu.VMEM)
    smem = pl.BlockSpec(memory_space=pltpu.SMEM)
    dma = pltpu.SemaphoreType.DMA
    return pl.pallas_call(
        functools.partial(kernel, n),
        out_shape=(out,) * 4,
        in_specs=[any_spec] * 4 + [smem] * 3,
        out_specs=(vmem,) * 4,
        scratch_shapes=[
            pltpu.VMEM((NCH, window, cols), BF),
            pltpu.VMEM((NCH, window, cols), BF),
            pltpu.VMEM((NCH, rows, cols), BF),
            pltpu.VMEM((NCH, rows, cols), BF),
            pltpu.VMEM((window, rows), F32),
            pltpu.VMEM((2, window, cols), F32),
            pltpu.VMEM((NCH, 2, rows, cols), F32),
            pltpu.VMEM((2, rows, cols), F32),
            pltpu.VMEM((NCH, 3, 2, rows, cols), BF),
            pltpu.VMEM((NCH, 4, 2, rows, cols), BF),
            pltpu.VMEM((NCH, 2, rows, cols), BF),
            dma((NCH, 2, 4)),
            dma((NCH, 2, 4, 2)),
            dma((NCH, 2, 4, 2)),
            dma((NCH, 2, 4, 2)),
            dma((NCH, 2, 4, 2)),
        ],
        compiler_params=pltpu.CompilerParams(
            collective_id=0, has_side_effects=True, vmem_limit_bytes=56 * 1024 * 1024
        ),
        name="attention",
    )(queries, keys, values, cotangent, local_blocks, far_blocks, counts)


def solution(mesh):
    rows = P(("groups", "seq"), None)
    return jax.shard_map(
        body,
        mesh=mesh,
        in_specs=(rows, rows, rows, rows, P("groups", None), P("groups", None), P("groups")),
        out_specs=(rows,) * 4,
        check_vma=False,
    )
```

```python
import functools
import math

import jax
import jax.numpy as jnp
from jax import lax
from jax.experimental import pallas as pl
from jax.experimental.pallas import tpu as pltpu
from jax.sharding import PartitionSpec as P

HEADS = 16
BLK = 128
MESH = pl.DeviceIdType.MESH
OFF = -1e30
NCH = 2
BF = jnp.bfloat16
F32 = jnp.float32


def dot_nt(a, b):
    return lax.dot_general(a, b, (((1,), (1,)), ((), ())), preferred_element_type=F32)


def dot_nn(a, b):
    return lax.dot_general(a, b, (((1,), (0,)), ((), ())), preferred_element_type=F32)


def dot_tn(a, b):
    return lax.dot_general(a, b, (((0,), (0,)), ((), ())), preferred_element_type=F32)


def kernel(
    n, q_hbm, k_hbm, v_hbm, g_hbm, local_ref, far_ref, counts_ref,
    o_ref, dq_ref, dk_ref, dv_ref,
    kbuf, vbuf, qbuf, gbuf, bias, acc, own, oacc, gsend, grecv,
    transit, own_sem, kv_send, kv_recv, gr_send, gr_recv,
):
    d = lax.axis_index("seq")
    place4 = lax.rem(d, 4)
    r0, r1, r2, r3 = (place4 == i for i in range(4))
    even = r0 | r2
    odd = r1 | r3
    rows, width = q_hbm.shape
    cols = width // NCH
    head = width // HEADS
    hpc = HEADS // NCH
    blocks = rows // BLK
    nblk = counts_ref.shape[0]
    hbm = (k_hbm, v_hbm)
    bufs = (kbuf, vbuf)
    scale = 1.0 / math.sqrt(head)
    early = 4
    cut = -(-(early * head) // 128) * 128
    spans = ((0, cut), (cut, cols - cut))

    def slot(a, c, s):
        return bufs[a].at[c, pl.ds(s * rows, rows), :]

    def span(ref, p):
        return ref.at[:, pl.ds(spans[p][0], spans[p][1])]

    def part(ref, c, p):
        return ref.at[:, pl.ds(pl.multiple_of(c * cols + spans[p][0], 128), spans[p][1])]

    def own_copies(c, p):
        out = []
        for i, (src, dst) in enumerate(
            ((k_hbm, slot(0, c, 2)), (v_hbm, slot(1, c, 2)), (q_hbm, qbuf.at[c]), (g_hbm, gbuf.at[c]))
        ):
            out.append(pltpu.make_async_copy(part(src, c, p), span(dst, p), own_sem.at[c, p, i]))
        return out

    def remote(src, dst, send, recv, delta):
        return pltpu.make_async_remote_copy(
            src_ref=src, dst_ref=dst, send_sem=send, recv_sem=recv,
            device_id={"seq": d + delta}, device_id_type=MESH,
        )

    def landing(place, a, c, p):
        return span(transit.at[c, a] if place == 3 else slot(a, c, (0, 1, 3)[place]), p)

    def kv_send_all(kind, src_place, dst_place, delta, c, p):
        for a in range(2):
            src = part(hbm[a], c, p) if src_place is None else landing(src_place, a, c, p)
            remote(
                src, landing(dst_place, a, c, p), kv_send.at[c, p, kind, a],
                kv_recv.at[c, p, dst_place, a], delta,
            ).start()

    def kv_wait(place, c, p):
        for a in range(2):
            there = landing(place, a, c, p)
            remote(there, there, kv_send.at[c, p, 0, a], kv_recv.at[c, p, place, a], 0).wait_recv()

    def kv_wait_send(kind, c, p):
        for a in range(2):
            there = landing(0, a, c, p)
            remote(there, there, kv_send.at[c, p, kind, a], kv_recv.at[c, p, 0, a], 0).wait_send()

    def gr_send_all(kind, place, delta, c, p):
        for a in range(2):
            src = grecv.at[c, 2, a] if kind == 3 else gsend.at[c, kind, a]
            remote(
                span(src, p), span(grecv.at[c, place, a], p), gr_send.at[c, p, kind, a],
                gr_recv.at[c, p, place, a], delta,
            ).start()

    def gr_wait(place, c, p):
        for a in range(2):
            there = span(grecv.at[c, place, a], p)
            remote(there, there, gr_send.at[c, p, 0, a], gr_recv.at[c, p, place, a], 0).wait_recv()

    def gr_wait_send(kind, c, p):
        for a in range(2):
            there = span(grecv.at[c, 0, a], p)
            remote(there, there, gr_send.at[c, p, kind, a], gr_recv.at[c, p, 0, a], 0).wait_send()

    has_prev = d >= 1
    has_prev2 = d >= 2
    has_next = d + 1 < n
    low4 = d >= 4
    up4 = d + 4 < n
    up3 = d + 3 < n
    in_cond = (has_prev2, has_prev, has_next)
    k2_cond = (r0 & up4) | (r1 & up3) | (r2 & low4)
    k3_cond = (r0 & low4) | r2
    kv_cond = (even | odd, jnp.logical_not(r3) | has_next, k2_cond, k3_cond)

    barrier = pltpu.get_barrier_semaphore()
    total = 0
    for delta, who in (
        (1, r0 | r1 | r2), (-1, r1 | r2 | r3), (2, r0), (-2, r2),
        (3, r0 | r1 | r3), (-3, r0 | r2 | r3), (4, r0), (-4, r0),
    ):
        cond = who & (d + delta >= 0) & (d + delta < n)
        total = total + cond.astype(jnp.int32)

        @pl.when(cond)
        def _(delta=delta):
            pl.semaphore_signal(barrier, inc=1, device_id={"seq": d + delta}, device_id_type=MESH)

    def start_own(c, carry):
        for p in range(2):
            for copy in own_copies(c, p):
                copy.start()
        return carry

    lax.fori_loop(0, NCH, start_own, 0)
    pl.semaphore_wait(barrier, total)

    def start_kv(c, carry):
        for p in range(2):
            pl.when(r0)(lambda: kv_send_all(1, None, 0, 2, c, p))
            pl.when(r1)(lambda: kv_send_all(1, None, 1, 1, c, p))
            pl.when(r2)(lambda: kv_send_all(1, None, 2, -1, c, p))
            pl.when(r3 & has_next)(lambda: kv_send_all(1, None, 3, -3, c, p))
            pl.when(even)(lambda: kv_send_all(0, None, 1, 1, c, p))
            pl.when(odd)(lambda: kv_send_all(0, None, 2, -1, c, p))
        return carry

    lax.fori_loop(0, NCH, start_kv, 0)

    def hand_on(c, p):
        @pl.when(r0 & up4)
        def _():
            kv_wait(3, c, p)
            kv_send_all(2, 3, 1, 4, c, p)

        @pl.when(r1)
        def _():
            kv_wait(2, c, p)
            pl.when(up3)(lambda: kv_send_all(2, 2, 0, 3, c, p))

        @pl.when(r2)
        def _():
            kv_wait(0, c, p)
            pl.when(low4)(lambda: kv_send_all(2, 0, 2, -3, c, p))
            kv_wait(1, c, p)
            kv_send_all(3, 1, 0, 1, c, p)

    def arrive(c, p):
        @pl.when(r0 & low4)
        def _():
            kv_wait(1, c, p)
            kv_send_all(3, 1, 0, 1, c, p)
            kv_wait(0, c, p)
        pl.when(even)(lambda: kv_wait(2, c, p))
        pl.when(odd)(lambda: kv_wait(1, c, p))
        pl.when(odd & has_prev2)(lambda: kv_wait(0, c, p))
        pl.when(r3 & has_next)(lambda: kv_wait(2, c, p))
        for copy in own_copies(c, p):
            copy.wait()

    def add_in(kind, place, c, p):
        at = pl.ds(spans[p][0], spans[p][1])
        gr_wait(place, c, p)
        for a in range(2):
            gsend[c, kind, a, :, at] = (
                gsend[c, kind, a, :, at].astype(F32) + grecv[c, place, a, :, at].astype(F32)
            ).astype(BF)

    def emit(c, p):
        at = pl.ds(spans[p][0], spans[p][1])
        for a in range(2):
            f = scale if a == 0 else 1.0
            for kind, s in ((0, 0), (1, 1), (2, 3)):
                gsend[c, kind, a, :, at] = (acc[a, pl.ds(s * rows, rows), at] * f).astype(BF)
            own[c, a, :, at] = acc[a, pl.ds(2 * rows, rows), at] * f
        pl.when(r0 & low4)(lambda: gr_send_all(0, 2, -3, c, p))
        pl.when(odd & has_prev2)(lambda: gr_send_all(0, 3, -1, c, p))
        pl.when(r3 & has_next)(lambda: gr_send_all(2, 2, 3, c, p))
        pl.when(even)(lambda: gr_send_all(2, 0, 1, c, p))
        pl.when(odd)(lambda: gr_send_all(1, 0, -1, c, p))

    def combine_core(c, p):
        @pl.when(r0 & low4)
        def _():
            add_in(1, 3, c, p)
            gr_send_all(1, 2, -4, c, p)

        @pl.when(r2)
        def _():
            add_in(1, 3, c, p)
            gr_send_all(1, 1, -1, c, p)

    def combine_chip(c, p):
        @pl.when(r1)
        def _():
            pl.when(up3)(lambda: add_in(2, 2, c, p))
            gr_send_all(2, 1, 1, c, p)

        @pl.when(r2)
        def _():
            pl.when(low4)(lambda: add_in(0, 2, c, p))
            gr_send_all(0, 1, -2, c, p)

    def pass_back(c, p):
        @pl.when(r0 & up4)
        def _():
            gr_wait(2, c, p)
            gr_send_all(3, 1, 3, c, p)

    hand_on(0, 0)

    for place, s in ((0, 0), (1, 1), (2, 3)):
        @pl.when(jnp.logical_not(in_cond[place]))
        def _(s=s):
            for a in range(2):
                for c in range(NCH):
                    bufs[a][c, pl.ds(s * rows, rows), :] = jnp.zeros((rows, cols), BF)

    position = lax.broadcasted_iota(jnp.int32, (BLK, BLK), 0)
    first = d * blocks
    for e in range(4 * blocks):
        index = first - 2 * blocks + e
        inside = (index >= 0) & (index < nblk)
        count = counts_ref[jnp.clip(index, 0, nblk - 1)]
        for a in range(blocks):
            listed = local_ref[0, first + a] == index
            for s in range(1, local_ref.shape[0]):
                listed = listed | (local_ref[s, first + a] == index)
            for s in range(far_ref.shape[0]):
                listed = listed | (far_ref[s, first + a] == index)
            live = jnp.where(listed & inside, count, 0)
            bias[pl.ds(e * BLK, BLK), pl.ds(a * BLK, BLK)] = jnp.where(position < live, 0.0, OFF)

    hand_on(0, 1)

    def compute(c):
        done = set()
        for h in range(hpc):
            if h == 0:
                arrive(c, 0)
            if h == 1:
                pl.when(c == 1)(lambda: combine_core(0, 1))
            if h == 2:
                pl.when(c == 1)(lambda: combine_chip(0, 0))
            if h == early:
                pl.when(c == 0)(lambda: hand_on(1, 0))
                pl.when(c == 1)(lambda: pass_back(0, 0))
                arrive(c, 1)
            if h == early + 1:
                emit(c, 0)
                pl.when(c == 0)(lambda: hand_on(1, 1))
                pl.when(c == 1)(lambda: combine_chip(0, 1))
            if h == early + 2:
                pl.when(c == 1)(lambda: pass_back(0, 1))
            if h == early + 3:
                combine_core(c, 0)
            low = h * head
            w0 = low // 128 * 128
            w1 = -(-(low + head) // 128) * 128
            w = w1 - w0
            lane = lax.broadcasted_iota(jnp.int32, (1, w), 1) + w0
            inhead = ((lane >= low) & (lane < low + head)).astype(F32)
            inhead_b = inhead.astype(BF)
            win = pl.ds(w0, w)
            qm = qbuf[c, :, win] * inhead_b
            gm = gbuf[c, :, win] * inhead_b
            kw = kbuf[c, :, win]
            vw = vbuf[c, :, win]
            s = dot_nt(kw, qm) * (scale * math.log2(math.e)) + bias[...]
            peak = jnp.max(s, axis=0, keepdims=True)
            e = jnp.exp2(s - peak)
            inv = 1.0 / jnp.sum(e, axis=0, keepdims=True)
            p = e * inv
            dp = dot_nt(vw, gm)
            delta = jnp.sum(p * dp, axis=0, keepdims=True)
            pb = p.astype(BF)
            ds = (p * (dp - delta)).astype(BF)
            terms = (
                (oacc, 0, dot_tn(pb, vw) * inhead),
                (oacc, 1, dot_tn(ds, kw) * inhead),
                (acc, 0, dot_nn(ds, qm)),
                (acc, 1, dot_nn(pb, gm)),
            )
            for ref, i, term in terms:
                for t in range(w0, w1, 128):
                    piece = term[:, t - w0 : t - w0 + 128]
                    at = pl.ds(t, 128)
                    if t in done:
                        ref[i, :, at] += piece
                    else:
                        ref[i, :, at] = piece
            done.update(range(w0, w1, 128))
        at = pl.ds(pl.multiple_of(c * cols, 128), cols)
        o_ref[:, at] = oacc[0].astype(BF)
        dq_ref[:, at] = (oacc[1] * scale).astype(BF)

    def chunk(c, carry):
        compute(c)
        emit(c, 1)
        return carry

    lax.fori_loop(0, NCH, chunk, 0)

    combine_core(1, 1)
    combine_chip(1, 0)
    pass_back(1, 0)
    combine_chip(1, 1)

    def finish(c, carry):
        pl.when(c == 1)(lambda: pass_back(1, 1))
        at = pl.ds(pl.multiple_of(c * cols, 128), cols)
        for p in range(2):
            gr_wait(0, c, p)
            pl.when(jnp.logical_not(r3) | has_next)(lambda: gr_wait(1, c, p))
        for a, ref in ((0, dk_ref), (1, dv_ref)):
            mine = own[c, a] + grecv[c, 0, a].astype(F32)
            other = grecv[c, 1, a].astype(F32)
            ref[:, at] = (mine + jnp.where(jnp.logical_not(r3) | has_next, other, 0.0)).astype(BF)
        for p in range(2):
            for kind in range(4):
                pl.when(kv_cond[kind])(lambda: kv_wait_send(kind, c, p))
            for kind, cond in ((0, has_prev2), (1, has_prev), (2, has_next), (3, r0 & up4)):
                pl.when(cond)(lambda: gr_wait_send(kind, c, p))
        return carry

    lax.fori_loop(0, NCH, finish, 0)


def body(queries, keys, values, cotangent, local_blocks, far_blocks, counts):
    rows, width = queries.shape
    cols = width // NCH
    n = lax.axis_size("seq")
    window = 4 * rows
    out = jax.ShapeDtypeStruct((rows, width), BF)
    any_spec = pl.BlockSpec(memory_space=pl.ANY)
    vmem = pl.BlockSpec(memory_space=pltpu.VMEM)
    smem = pl.BlockSpec(memory_space=pltpu.SMEM)
    dma = pltpu.SemaphoreType.DMA
    return pl.pallas_call(
        functools.partial(kernel, n),
        out_shape=(out,) * 4,
        in_specs=[any_spec] * 4 + [smem] * 3,
        out_specs=(vmem,) * 4,
        scratch_shapes=[
            pltpu.VMEM((NCH, window, cols), BF),
            pltpu.VMEM((NCH, window, cols), BF),
            pltpu.VMEM((NCH, rows, cols), BF),
            pltpu.VMEM((NCH, rows, cols), BF),
            pltpu.VMEM((window, rows), F32),
            pltpu.VMEM((2, window, cols), F32),
            pltpu.VMEM((NCH, 2, rows, cols), F32),
            pltpu.VMEM((2, rows, cols), F32),
            pltpu.VMEM((NCH, 3, 2, rows, cols), BF),
            pltpu.VMEM((NCH, 4, 2, rows, cols), BF),
            pltpu.VMEM((NCH, 2, rows, cols), BF),
            dma((NCH, 2, 4)),
            dma((NCH, 2, 4, 2)),
            dma((NCH, 2, 4, 2)),
            dma((NCH, 2, 4, 2)),
            dma((NCH, 2, 4, 2)),
        ],
        compiler_params=pltpu.CompilerParams(
            collective_id=0, has_side_effects=True, vmem_limit_bytes=56 * 1024 * 1024
        ),
        name="attention",
    )(queries, keys, values, cotangent, local_blocks.T, far_blocks.T, counts)


def solution(mesh):
    rows = P(("groups", "seq"), None)
    return jax.shard_map(
        body,
        mesh=mesh,
        in_specs=(rows, rows, rows, rows, P("groups", None), P("groups", None), P("groups")),
        out_specs=(rows,) * 4,
        check_vma=False,
    )
```
